512 devices in a mesh: region: 8 (over x, y_hi), pos: 64 (over z, y_lo, core).
Axes of the slice: x: 4, y: 4 (y_hi: 2, y_lo: 2; y = y_hi * 2 + y_lo), z: 16, core: 2. Of those that a mesh axis runs over, the one named last changes fastest.
Arguments:
- object_real: bfloat16 [3, 2048, 256], P(None, ('region', 'pos')), may hold values from 0.5 to 1.5
- object_imag: bfloat16 [3, 2048, 256], P(None, ('region', 'pos')), may hold values from -1.1953125 to 1.1953125
- probe_real: float32 [128, 128], replicated, may hold values from -4 to 4
- probe_imag: float32 [128, 128], replicated, may hold values from -4 to 4
- patterns: bfloat16 [8, 768, 128, 128], P('region', 'pos'), may hold values from 0 to 2
- offsets: int32 [8, 768, 2], P('region', 'pos'), may hold values from 0 to 255, as said below
- counts: int32 [8, 64], P('region', 'pos'), may hold values from 1 to 12, as said below
Outputs:
- grad_real: float32 [3, 2048, 256], P(None, ('region', 'pos'))
- grad_imag: float32 [3, 2048, 256], P(None, ('region', 'pos'))
The draws below stay inside these ranges and needn't reach their ends.
Inputs may be any that keep to these rules, and one draw needn't show every extreme that they name: offsets[..., 0] lies in 0..255 and reaches 255 in every draw; offsets[..., 1] lies in 0..128. `counts`: every device has at least one live slot; some device has all 12 live in every draw.
All inputs are finite; a program needn't handle non-finite values.
Results may differ from the reference program's by a relative error of at most 0.0024.
Values may be sent and summed in bfloat16 or wider, within the bound.
No kernel may reach another device: no remote copies, remote signals or barrier semaphores. Data moves between devices by JAX's collectives and lax.ppermute only.
A program may use at most 64 MiB of HBM per device.

```python
import math
import jax
import jax.numpy as jnp
from jax import lax

P_SIZE = 128
SLICES = 3
SLOTS = 12
REGION_ROWS = 256
COLS = 256
REGIONS = 8
POSITIONS = 768
ROWS = 2048
N_POS = 64


def draw_offsets(key, part):
    key = jax.random.fold_in(key, 3)
    key_rows, key_cols, key_place = jax.random.split(key, 3)
    total = REGIONS * POSITIONS
    rows = jax.random.randint(key_rows, (total,), 0, REGION_ROWS)
    place = jax.random.randint(key_place, (), 0, total)
    rows = rows.at[place].set(REGION_ROWS - 1)
    cols = jax.random.randint(key_cols, (total,), 0, COLS - P_SIZE + 1)
    return jnp.stack([rows, cols], axis=1).reshape(REGIONS, POSITIONS, 2).astype(jnp.int32)


def draw_counts(key, part):
    key = jax.random.fold_in(key, 7)
    key_vals, key_place = jax.random.split(key)
    total = REGIONS * N_POS
    values = jax.random.randint(key_vals, (total,), 1, SLOTS + 1)
    place = jax.random.randint(key_place, (), 0, total)
    values = values.at[place].set(SLOTS)
    return values.reshape(REGIONS, N_POS).astype(jnp.int32)


def level_of(own_key, dims, pieces, least, high):
    factor_of = 1.0
    for position, parts in pieces:
        draws = jax.random.uniform(jax.random.fold_in(jax.random.fold_in(own_key, 6), position), (parts,), jnp.float32, least / len(pieces), high / len(pieces))
        factor_of = factor_of * jnp.repeat(jnp.exp(draws), dims[position] // parts).reshape((-1,) + (1,) * (len(dims) - 1 - position))
    return factor_of


def centred(rng, shape, deviation, reach, shards=(), kind=jnp.bfloat16):
    result = deviation * jax.random.normal(rng, shape, jnp.float32)
    if shards:
        result = result * level_of(rng, shape, shards, -0.22, 0.18)
    return jnp.clip(result, -reach, reach).astype(kind)


def setup_inputs(seed: int = 0) -> dict:
    key_list = jax.random.split(jax.random.key(seed), 8)
    return {
        "object_real": jnp.clip(1.0 + 0.1 * jax.random.normal(key_list[0], (SLICES, ROWS, COLS), jnp.float32), 0.5, 1.5).astype(jnp.bfloat16),
        "object_imag": centred(key_list[1], (SLICES, ROWS, COLS), 0.3, 1.1953125, ((1, 512),)),
        "probe_real": centred(key_list[2], (P_SIZE, P_SIZE), 0.7, 4.0, (), jnp.float32),
        "probe_imag": centred(key_list[3], (P_SIZE, P_SIZE), 0.7, 4.0, (), jnp.float32),
        "patterns": jnp.clip(2.0 * jax.random.uniform(key_list[4], (REGIONS, POSITIONS, P_SIZE, P_SIZE), jnp.float32) ** level_of(key_list[4], (REGIONS, POSITIONS, P_SIZE, P_SIZE), ((0, 8), (1, 64)), -0.2, 0.2), 0.0, 2.0).astype(jnp.bfloat16),
        "offsets": draw_offsets(jax.random.fold_in(key_list[7], 71), 0),
        "counts": draw_counts(jax.random.fold_in(key_list[7], 71), 0),
    }


FRESNEL = 12.0

def fresnel_kernel():
    freq = jnp.fft.fftfreq(P_SIZE).astype(jnp.float32)
    phase = -jnp.pi * FRESNEL * (freq[:, None] * freq[:, None] + freq[None, :] * freq[None, :])
    return jnp.exp(1j * phase)

def propagate(field, kernel):
    return jnp.fft.ifft2(kernel * jnp.fft.fft2(field, norm='ortho'), norm='ortho')

def patch_gradient(layers, probe, measured, kernel):
    waves = []
    wave = probe
    exit_wave = probe
    for layer in range(SLICES):
        waves.append(wave)
        exit_wave = wave * layers[layer]
        if layer < SLICES - 1:
            wave = propagate(exit_wave, kernel)
    farfield = jnp.fft.fft2(exit_wave, norm='ortho')
    intensity = jnp.real(farfield) * jnp.real(farfield) + jnp.imag(farfield) * jnp.imag(farfield)
    backward = jnp.fft.ifft2((intensity - measured) * farfield, norm='ortho')
    grads = [None] * SLICES
    for layer in range(SLICES - 1, -1, -1):
        grads[layer] = jnp.conj(waves[layer]) * backward
        if layer > 0:
            backward = propagate(jnp.conj(layers[layer]) * backward, jnp.conj(kernel))
    return jnp.stack(grads)

def reference(object_real, object_imag, probe_real, probe_imag, patterns, offsets, counts):
    rows_all = REGIONS * REGION_ROWS
    wide_real = jnp.concatenate([object_real, object_real[:, :P_SIZE]], axis=1).astype(jnp.float32)
    wide_imag = jnp.concatenate([object_imag, object_imag[:, :P_SIZE]], axis=1).astype(jnp.float32)
    field = wide_real + 1j * wide_imag
    probe = probe_real + 1j * probe_imag
    kernel = fresnel_kernel()
    scale = 1.0 / math.sqrt(SLOTS * N_POS)

    def visit(index, carry):
        grad_real, grad_imag = carry
        region = index // POSITIONS
        slot = index % POSITIONS
        device = slot // SLOTS
        within = slot % SLOTS
        live = (within < counts[region, device]).astype(jnp.float32)
        row = (region * REGION_ROWS + offsets[region, slot, 0]).astype(jnp.int32)
        column = offsets[region, slot, 1].astype(jnp.int32)
        start = (jnp.int32(0), row, column)
        layers = lax.dynamic_slice(field, start, (SLICES, P_SIZE, P_SIZE))
        measured = patterns[region, slot].astype(jnp.float32)
        gradient = patch_gradient(layers, probe, measured, kernel) * (live * scale)
        old_real = lax.dynamic_slice(grad_real, start, (SLICES, P_SIZE, P_SIZE))
        old_imag = lax.dynamic_slice(grad_imag, start, (SLICES, P_SIZE, P_SIZE))
        grad_real = lax.dynamic_update_slice(grad_real, old_real + jnp.real(gradient), start)
        grad_imag = lax.dynamic_update_slice(grad_imag, old_imag + jnp.imag(gradient), start)
        return (grad_real, grad_imag)
    zeros = jnp.zeros((SLICES, rows_all + P_SIZE, COLS), jnp.float32)
    grad_real, grad_imag = lax.fori_loop(0, REGIONS * POSITIONS, visit, (zeros, zeros))
    final_real = grad_real[:, :rows_all].at[:, :P_SIZE].add(grad_real[:, rows_all:])
    final_imag = grad_imag[:, :rows_all].at[:, :P_SIZE].add(grad_imag[:, rows_all:])
    return (final_real, final_imag)
```

```python
import functools
import math

import jax
import jax.numpy as jnp
import numpy as np
from jax import lax
from jax.experimental import pallas as pl
from jax.experimental.pallas import tpu as pltpu
from jax.sharding import Mesh
from jax.sharding import PartitionSpec as P

FRESNEL = 12.0
GROUP = 4
PROP, DFT = 0, 2
POS = ("z", "yl", "core")


def block_tables(width):
    index = np.arange(width)
    turns = index[:, None] * index[None, :] % width
    dft = np.exp(-2j * np.pi * turns / width) / np.sqrt(width)
    freq = np.fft.fftfreq(width)
    phase = np.exp(-1j * np.pi * FRESNEL * freq * freq)
    prop = np.conj(dft) @ (phase[:, None] * dft)
    pieces = []
    for matrix in (prop, dft):
        right = np.block([[matrix.real, matrix.imag], [-matrix.imag, matrix.real]])
        for table in (right, right.T):
            high = table.astype(np.float32).astype(jnp.bfloat16)
            low = (table - high.astype(np.float64)).astype(np.float32).astype(jnp.bfloat16)
            pieces.append(np.stack([high, low]))
    return np.stack(pieces)


def split(value):
    high = value.astype(jnp.bfloat16)
    low = (value - high.astype(jnp.float32)).astype(jnp.bfloat16)
    return high, low


def dot(first, second):
    return jnp.dot(first, second, preferred_element_type=jnp.float32)


def left(table_ref, which, real, imag):
    field = jnp.concatenate(
        [jnp.concatenate(real, axis=1), jnp.concatenate(imag, axis=1)], axis=0
    )
    high, low = split(field)
    table_high, table_low = table_ref[which, 0], table_ref[which, 1]
    out = dot(table_high, high) + dot(table_low, high) + dot(table_high, low)
    w = real[0].shape[0]
    spans = [slice(k * w, (k + 1) * w) for k in range(len(real))]
    return [out[:w, s] for s in spans], [out[w:, s] for s in spans]


def right(table_ref, which, real, imag):
    field = jnp.concatenate(
        [jnp.concatenate([r, i], axis=1) for r, i in zip(real, imag)], axis=0
    )
    high, low = split(field)
    table_high, table_low = table_ref[which, 0], table_ref[which, 1]
    out = dot(high, table_high) + dot(high, table_low) + dot(low, table_high)
    w = real[0].shape[0]
    spans = [slice(k * w, (k + 1) * w) for k in range(len(real))]
    return [out[s, :w] for s in spans], [out[s, w:] for s in spans]


def transform(table_ref, base, adjoint, field):
    flip = 1 if adjoint else 0
    return right(table_ref, base + flip, *left(table_ref, base + 1 - flip, *field))


def mul(first, second):
    real = [p * r - q * s for p, q, r, s in zip(*first, *second)]
    imag = [p * s + q * r for p, q, r, s in zip(*first, *second)]
    return real, imag


def conj_mul(first, second):
    real = [p * r + q * s for p, q, r, s in zip(*first, *second)]
    imag = [p * s - q * r for p, q, r, s in zip(*first, *second)]
    return real, imag


def slots_kernel(
    scale,
    place_ref,
    off_ref,
    cnt_ref,
    probe_real_ref,
    probe_imag_ref,
    pat_ref,
    tab_ref,
    own_near_ref,
    own_far_ref,
    next_near_ref,
    next_far_ref,
    keep_ref,
    send_ref,
    keep_next_ref,
    send_next_ref,
    obj_ref,
    grad_ref,
):
    w = probe_real_ref.shape[0]
    slots = pat_ref.shape[0]
    slices = obj_ref.shape[1]
    half = 4
    yl = place_ref[0]
    first_core = place_ref[1] == 0
    grad_ref[...] = jnp.zeros_like(grad_ref)
    top = lax.broadcasted_iota(jnp.int32, (2 * half, w), 0) < half

    def unpack(near_ref, far_ref, first_row):
        def place(z, _):
            for y in range(2):
                row = first_row + (2 * z + lax.rem(y + yl, 2)) * 2 * half
                row = pl.multiple_of(row, 2 * half)
                near = near_ref[y, z].astype(jnp.float32)
                far = far_ref[y, z].astype(jnp.float32)
                low = jnp.where(first_core, near, far)
                high = jnp.where(first_core, far, near)
                for s in range(slices):
                    for h in range(2):
                        k = (s * 2 + h) * 2 * half
                        a, b = low[k : k + 2 * half], high[k : k + 2 * half]
                        obj_ref[0, s, h, pl.ds(row, 2 * half), :] = jnp.where(
                            top, a, pltpu.roll(b, half, 0)
                        )
                        obj_ref[1, s, h, pl.ds(row, 2 * half), :] = jnp.where(
                            top, pltpu.roll(a, half, 0), b
                        )
            return 0

        lax.fori_loop(0, near_ref.shape[1], place, 0)

    def pack(keep_out, send_out, first_row):
        def place(z, _):
            for y in range(2):
                row = first_row + (2 * z + lax.rem(y + yl, 2)) * 2 * half
                row = pl.multiple_of(row, 2 * half)
                for s in range(slices):
                    for h in range(2):
                        k = (s * 2 + h) * 2 * half
                        real = grad_ref[0, s, h, pl.ds(row, 2 * half), :]
                        imag = grad_ref[1, s, h, pl.ds(row, 2 * half), :]
                        low = jnp.where(top, real, pltpu.roll(imag, half, 0))
                        high = jnp.where(top, pltpu.roll(real, half, 0), imag)
                        keep_out[y, z, k : k + 2 * half] = jnp.where(first_core, low, high)
                        send_out[y, z, k : k + 2 * half] = jnp.where(first_core, high, low)
            return 0

        lax.fori_loop(0, keep_out.shape[1], place, 0)

    band_rows = own_near_ref.shape[1] * 4 * half
    unpack(own_near_ref, own_far_ref, 0)
    unpack(next_near_ref, next_far_ref, band_rows)

    count = cnt_ref[0, 0]
    lane = lax.broadcasted_iota(jnp.int32, (w, w), 1)

    def visit(step, _):
        numbers = [jnp.minimum(step * GROUP + k, slots - 1) for k in range(GROUP)]
        rows = [off_ref[0, n, 0] for n in numbers]
        cols = [off_ref[0, n, 1] for n in numbers]
        weights = [
            jnp.where(step * GROUP + k < count, scale, 0.0).astype(jnp.float32)
            for k in range(GROUP)
        ]
        turn = [lax.rem(c, w) for c in cols]
        back_turn = [lax.rem(2 * w - c, w) for c in cols]

        def window(part, layer):
            found = []
            for k in range(GROUP):
                near = obj_ref[part, layer, 0, pl.ds(rows[k], w), :]
                after = obj_ref[part, layer, 1, pl.ds(rows[k], w), :]
                found.append(pltpu.roll(jnp.where(lane >= cols[k], near, after), back_turn[k], 1))
            return found

        layers = [(window(0, s), window(1, s)) for s in range(slices)]
        wave = ([probe_real_ref[...]] * GROUP, [probe_imag_ref[...]] * GROUP)
        waves = []
        for s in range(slices):
            waves.append(wave)
            leaving = mul(wave, layers[s])
            if s < slices - 1:
                wave = transform(tab_ref, PROP, False, leaving)
        far = transform(tab_ref, DFT, False, leaving)
        misfit = [
            r * r + i * i - pat_ref[n].astype(jnp.float32) for r, i, n in zip(*far, numbers)
        ]
        back = ([m * r for m, r in zip(misfit, far[0])], [m * i for m, i in zip(misfit, far[1])])
        back = transform(tab_ref, DFT, True, back)
        for s in range(slices - 1, -1, -1):
            term = conj_mul(waves[s], back)
            for part in range(2):
                for k in range(GROUP):
                    moved = pltpu.roll(term[part][k] * weights[k], turn[k], 1)
                    here = lane >= cols[k]
                    grad_ref[part, s, 0, pl.ds(rows[k], w), :] += jnp.where(here, moved, 0.0)
                    grad_ref[part, s, 1, pl.ds(rows[k], w), :] += jnp.where(here, 0.0, moved)
            if s > 0:
                back = transform(tab_ref, PROP, True, conj_mul(layers[s], back))
        return 0

    lax.fori_loop(0, lax.div(count + (GROUP - 1), GROUP), visit, 0)
    pack(keep_next_ref, send_next_ref, band_rows)
    pack(keep_ref, send_ref, 0)


def slots_call(scale, place, offsets, counts, probe, patterns, tables, own, following):
    slices = 3
    width = probe[0].shape[0]
    rows = (own[0].shape[1] + following[0].shape[1]) * 16
    vector = pl.BlockSpec(memory_space=pltpu.VMEM)
    scalar = pl.BlockSpec(memory_space=pltpu.SMEM)
    held = pltpu.VMEM((2, slices, 2, rows, width), jnp.float32)
    outs = [jax.ShapeDtypeStruct(x.shape, jnp.float32) for x in (own[0],) * 2 + (following[0],) * 2]
    return pl.pallas_call(
        functools.partial(slots_kernel, scale),
        out_shape=outs,
        in_specs=[scalar] * 3 + [vector] * 8,
        out_specs=[vector] * 4,
        scratch_shapes=[held, held],
        compiler_params=pltpu.CompilerParams(vmem_limit_bytes=56 * 1024 * 1024),
        name="slots",
    )(place, offsets, counts, *probe, patterns, tables, *own, *following)


def swap(block, axis):
    return lax.ppermute(block, axis, [(0, 1), (1, 0)])


def shift(block, distance):
    bands = lax.axis_size("region")
    return lax.ppermute(block, "region", [(i, (i + distance) % bands) for i in range(bands)])


def local(tables, object_real, object_imag, probe_real, probe_imag, patterns, offsets, counts):
    slices, rows, columns = object_real.shape
    width = probe_real.shape[0]
    halves = columns // width
    depth = lax.axis_size("z")
    below = depth * width // (depth * 4 * rows)
    packed = slices * halves * 2 * rows
    yl = lax.axis_index("yl")
    place = jnp.stack([yl, lax.axis_index("core")]).astype(jnp.int32)
    scale = 1.0 / math.sqrt(patterns.shape[1] * depth * 4)

    with jax.named_scope("gather"):
        block = jnp.stack([object_real, object_imag]).reshape(2, slices, rows, halves, width)
        block = block.transpose(1, 3, 0, 2, 4).reshape(1, packed, width)
        column = lax.all_to_all(
            jnp.broadcast_to(block, (depth, packed, width)), "z", 0, 0, tiled=True
        )
        following = shift(column[:below], -1)
        other = swap(column, "yl")
        own = jnp.stack([column, other])
        own_far = swap(own, "core")
        following = jnp.stack([following, swap(following, "yl")])
        following_far = swap(following, "core")

    keep, send, keep_next, send_next = slots_call(
        scale,
        place,
        offsets,
        counts,
        (probe_real, probe_imag),
        patterns[0],
        tables,
        (own, own_far),
        (following, following_far),
    )

    with jax.named_scope("reduce"):
        carried = keep_next + swap(send_next, "core")
        total = keep + swap(send, "core")
        carried = carried[0] + swap(carried[1], "yl")
        total = total[0] + swap(total[1], "yl")
        total = total.at[:below].add(shift(carried, 1))
        total = lax.all_to_all(total, "z", 0, 0, tiled=True).sum(0)
        total = total.reshape(slices, halves, 2, rows, width).transpose(2, 0, 3, 1, 4)
        total = total.reshape(2, slices, rows, columns)
    return total[0], total[1]


def solution(mesh):
    fine = Mesh(mesh.devices.reshape(mesh.shape["region"], -1, 2, 2), ("region",) + POS)
    everything = ("region",) + POS
    run = jax.shard_map(
        local,
        mesh=fine,
        in_specs=(
            P(),
            P(None, everything, None),
            P(None, everything, None),
            P(),
            P(),
            P("region", POS, None, None),
            P("region", POS, None),
            P("region", POS),
        ),
        out_specs=(P(None, everything, None), P(None, everything, None)),
        check_vma=False,
    )

    def whole(object_real, object_imag, probe_real, probe_imag, patterns, offsets, counts):
        tables = jnp.asarray(block_tables(probe_real.shape[0]))
        return run(
            tables, object_real, object_imag, probe_real, probe_imag, patterns, offsets, counts
        )

    return whole
```

```python
import functools
import math

import jax
import jax.numpy as jnp
import numpy as np
from jax import lax
from jax.experimental import pallas as pl
from jax.experimental.pallas import tpu as pltpu
from jax.sharding import Mesh
from jax.sharding import PartitionSpec as P

FRESNEL = 12.0
GROUP = 4
PROP, DFT = 0, 2
POS = ("z", "yl", "core")


def block_tables(width):
    index = np.arange(width)
    turns = index[:, None] * index[None, :] % width
    dft = np.exp(-2j * np.pi * turns / width) / np.sqrt(width)
    freq = np.fft.fftfreq(width)
    phase = np.exp(-1j * np.pi * FRESNEL * freq * freq)
    prop = np.conj(dft) @ (phase[:, None] * dft)
    pieces = []
    for matrix in (prop, dft):
        right = np.block([[matrix.real, matrix.imag], [-matrix.imag, matrix.real]])
        for table in (right, right.T):
            high = table.astype(np.float32).astype(jnp.bfloat16)
            low = (table - high.astype(np.float64)).astype(np.float32).astype(jnp.bfloat16)
            pieces.append(np.stack([high, low]))
    return np.stack(pieces)


def split(value):
    high = value.astype(jnp.bfloat16)
    low = (value - high.astype(jnp.float32)).astype(jnp.bfloat16)
    return high, low


def dot(first, second):
    return jnp.dot(first, second, preferred_element_type=jnp.float32)


def left(table_ref, which, real, imag):
    field = jnp.concatenate(
        [jnp.concatenate(real, axis=1), jnp.concatenate(imag, axis=1)], axis=0
    )
    high, low = split(field)
    table_high, table_low = table_ref[which, 0], table_ref[which, 1]
    out = dot(table_high, high) + dot(table_low, high) + dot(table_high, low)
    w = real[0].shape[0]
    spans = [slice(k * w, (k + 1) * w) for k in range(len(real))]
    return [out[:w, s] for s in spans], [out[w:, s] for s in spans]


def right(table_ref, which, real, imag):
    field = jnp.concatenate(
        [jnp.concatenate([r, i], axis=1) for r, i in zip(real, imag)], axis=0
    )
    high, low = split(field)
    table_high, table_low = table_ref[which, 0], table_ref[which, 1]
    out = dot(high, table_high) + dot(high, table_low) + dot(low, table_high)
    w = real[0].shape[0]
    spans = [slice(k * w, (k + 1) * w) for k in range(len(real))]
    return [out[s, :w] for s in spans], [out[s, w:] for s in spans]


def transform(table_ref, base, adjoint, field):
    flip = 1 if adjoint else 0
    return right(table_ref, base + flip, *left(table_ref, base + 1 - flip, *field))


def mul(first, second):
    real = [p * r - q * s for p, q, r, s in zip(*first, *second)]
    imag = [p * s + q * r for p, q, r, s in zip(*first, *second)]
    return real, imag


def conj_mul(first, second):
    real = [p * r + q * s for p, q, r, s in zip(*first, *second)]
    imag = [p * s - q * r for p, q, r, s in zip(*first, *second)]
    return real, imag


def slots_kernel(
    scale,
    place_ref,
    off_ref,
    cnt_ref,
    probe_real_ref,
    probe_imag_ref,
    pat_ref,
    tab_ref,
    near_ref,
    far_ref,
    keep_ref,
    send_ref,
    obj_ref,
    grad_ref,
):
    w = probe_real_ref.shape[0]
    slots = pat_ref.shape[0]
    slices = obj_ref.shape[1]
    half = 4
    yl = place_ref[0]
    first_core = place_ref[1] == 0
    grad_ref[...] = jnp.zeros_like(grad_ref)
    top = lax.broadcasted_iota(jnp.int32, (2 * half, w), 0) < half

    def eight_rows(y, z):
        return pl.ds(pl.multiple_of((2 * z + lax.rem(y + yl, 2)) * 2 * half, 2 * half), 2 * half)

    def unpack(z, _):
        for y in range(2):
            rows = eight_rows(y, z)
            near = near_ref[y, z].astype(jnp.float32)
            far = far_ref[y, z].astype(jnp.float32)
            low = jnp.where(first_core, near, far)
            high = jnp.where(first_core, far, near)
            for s in range(slices):
                for h in range(2):
                    k = (s * 2 + h) * 2 * half
                    a, b = low[k : k + 2 * half], high[k : k + 2 * half]
                    obj_ref[0, s, h, rows, :] = jnp.where(top, a, pltpu.roll(b, half, 0))
                    obj_ref[1, s, h, rows, :] = jnp.where(top, pltpu.roll(a, half, 0), b)
        return 0

    def pack(z, _):
        for y in range(2):
            rows = eight_rows(y, z)
            for s in range(slices):
                for h in range(2):
                    k = (s * 2 + h) * 2 * half
                    real = grad_ref[0, s, h, rows, :]
                    imag = grad_ref[1, s, h, rows, :]
                    low = jnp.where(top, real, pltpu.roll(imag, half, 0))
                    high = jnp.where(top, pltpu.roll(real, half, 0), imag)
                    keep_ref[y, z, k : k + 2 * half] = jnp.where(first_core, low, high)
                    send_ref[y, z, k : k + 2 * half] = jnp.where(first_core, high, low)
        return 0

    blocks = near_ref.shape[1]
    lax.fori_loop(0, blocks, unpack, 0)

    count = cnt_ref[0, 0]
    lane = lax.broadcasted_iota(jnp.int32, (w, w), 1)

    def visit(step, _):
        numbers = [jnp.minimum(step * GROUP + k, slots - 1) for k in range(GROUP)]
        rows = [off_ref[0, n, 0] for n in numbers]
        cols = [off_ref[0, n, 1] for n in numbers]
        weights = [
            jnp.where(step * GROUP + k < count, scale, 0.0).astype(jnp.float32)
            for k in range(GROUP)
        ]
        turn = [lax.rem(c, w) for c in cols]
        back_turn = [lax.rem(2 * w - c, w) for c in cols]

        def window(part, layer):
            found = []
            for k in range(GROUP):
                near = obj_ref[part, layer, 0, pl.ds(rows[k], w), :]
                after = obj_ref[part, layer, 1, pl.ds(rows[k], w), :]
                found.append(pltpu.roll(jnp.where(lane >= cols[k], near, after), back_turn[k], 1))
            return found

        layers = [(window(0, s), window(1, s)) for s in range(slices)]
        wave = ([probe_real_ref[...]] * GROUP, [probe_imag_ref[...]] * GROUP)
        waves = []
        for s in range(slices):
            waves.append(wave)
            leaving = mul(wave, layers[s])
            if s < slices - 1:
                wave = transform(tab_ref, PROP, False, leaving)
        far = transform(tab_ref, DFT, False, leaving)
        misfit = [
            r * r + i * i - pat_ref[n].astype(jnp.float32) for r, i, n in zip(*far, numbers)
        ]
        back = ([m * r for m, r in zip(misfit, far[0])], [m * i for m, i in zip(misfit, far[1])])
        back = transform(tab_ref, DFT, True, back)
        for s in range(slices - 1, -1, -1):
            term = conj_mul(waves[s], back)
            for part in range(2):
                for k in range(GROUP):
                    moved = pltpu.roll(term[part][k] * weights[k], turn[k], 1)
                    here = lane >= cols[k]
                    grad_ref[part, s, 0, pl.ds(rows[k], w), :] += jnp.where(here, moved, 0.0)
                    grad_ref[part, s, 1, pl.ds(rows[k], w), :] += jnp.where(here, 0.0, moved)
            if s > 0:
                back = transform(tab_ref, PROP, True, conj_mul(layers[s], back))
        return 0

    lax.fori_loop(0, lax.div(count + (GROUP - 1), GROUP), visit, 0)
    lax.fori_loop(0, blocks, pack, 0)


def slots_call(scale, place, offsets, counts, probe, patterns, tables, near, far):
    slices = 3
    width = probe[0].shape[0]
    vector = pl.BlockSpec(memory_space=pltpu.VMEM)
    scalar = pl.BlockSpec(memory_space=pltpu.SMEM)
    held = pltpu.VMEM((2, slices, 2, near.shape[1] * 16, width), jnp.float32)
    return pl.pallas_call(
        functools.partial(slots_kernel, scale),
        out_shape=[jax.ShapeDtypeStruct(near.shape, jnp.float32)] * 2,
        in_specs=[scalar] * 3 + [vector] * 6,
        out_specs=[vector] * 2,
        scratch_shapes=[held, held],
        compiler_params=pltpu.CompilerParams(vmem_limit_bytes=40 * 1024 * 1024),
        name="slots",
    )(place, offsets, counts, *probe, patterns, tables, near, far)


def swap(block, axis):
    return lax.ppermute(block, axis, [(0, 1), (1, 0)])


def shift(block, distance):
    bands = lax.axis_size("region")
    return lax.ppermute(block, "region", [(i, (i + distance) % bands) for i in range(bands)])


def shift_and_swap(block, distance):
    bands = lax.axis_size("region")
    route = [(2 * i + y, (i + distance) % bands * 2 + 1 - y) for i in range(bands) for y in (0, 1)]
    return lax.ppermute(block, ("region", "yl"), route)


def encode(blocks, over):
    most = jnp.max(jnp.abs(blocks), axis=over, keepdims=True)
    code = jnp.ceil(jnp.log2(jnp.maximum(most, 1e-37)) * 64.0)
    share = jnp.clip(jnp.round(blocks * jnp.exp2(code / -64.0) * 32767.0), -32767.0, 32767.0)
    return share.astype(jnp.int16), code[0].astype(jnp.int16)


def decode(message, axis):
    code = lax.slice_in_dim(message, message.shape[axis] - 1, None, axis=axis)
    share = lax.slice_in_dim(message, 0, message.shape[axis] - 1, axis=axis)
    return share.astype(jnp.float32) * (jnp.exp2(code.astype(jnp.float32) / 64.0) / 32767.0)


def local(tables, object_real, object_imag, probe_real, probe_imag, patterns, offsets, counts):
    slices, rows, columns = object_real.shape
    width = probe_real.shape[0]
    halves = columns // width
    depth = lax.axis_size("z")
    below = width // (4 * rows)
    packed = slices * halves * 2 * rows
    place = jnp.stack([lax.axis_index("yl"), lax.axis_index("core")]).astype(jnp.int32)
    scale = 1.0 / math.sqrt(patterns.shape[1] * depth * 4)

    with jax.named_scope("gather"):
        block = jnp.stack([object_real, object_imag]).reshape(2, slices, rows, halves, width)
        block = block.transpose(1, 3, 0, 2, 4).reshape(packed, width)
        column = lax.all_to_all(
            jnp.broadcast_to(block, (depth, packed, width)), "z", 0, 0, tiled=True
        )
        other = swap(column, "yl")
        following = shift(column[:below], -1)
        following_other = shift_and_swap(column[:below], -1)
        near = jnp.concatenate([column, following, other, following_other])
        near = near.reshape(2, depth + below, packed, width)
        far = swap(near, "core")

    keep, send = slots_call(
        scale, place, offsets, counts, (probe_real, probe_imag), patterns[0], tables, near, far
    )

    with jax.named_scope("reduce"):
        total = keep + swap(send, "core")
        away = jnp.concatenate([total[1], total[0, depth:]])
        share, code = encode(away, (0,))
        code = code[None]
        near_next = jnp.concatenate([share[depth + below :], code])
        far_next = jnp.concatenate([share[depth : depth + below], code])
        beside = jnp.concatenate([share[:depth], code])
        far_next = shift_and_swap(far_next, 1)
        near_next = shift(near_next, 1)
        beside = swap(beside, "yl")
        total = total[0, :depth] + decode(beside, 0)
        total = total.at[:below].add(decode(near_next, 0) + decode(far_next, 0))
        total = total.reshape(depth, -1, 2 * rows, width)
        share, code = encode(total, (0, 1))
        code = jnp.broadcast_to(code, (depth,) + code.shape)
        message = jnp.concatenate([share, code], axis=1).reshape(depth, -1, width)
        message = lax.all_to_all(message, "z", 0, 0, tiled=True)
        total = decode(message.reshape(depth, -1, 2 * rows, width), 1).sum(0)
        total = total.reshape(slices, halves, 2, rows, width).transpose(2, 0, 3, 1, 4)
        total = total.reshape(2, slices, rows, columns)
    return total[0], total[1]


def solution(mesh):
    fine = Mesh(mesh.devices.reshape(mesh.shape["region"], -1, 2, 2), ("region",) + POS)
    everything = ("region",) + POS
    run = jax.shard_map(
        local,
        mesh=fine,
        in_specs=(
            P(),
            P(None, everything, None),
            P(None, everything, None),
            P(),
            P(),
            P("region", POS, None, None),
            P("region", POS, None),
            P("region", POS),
        ),
        out_specs=(P(None, everything, None), P(None, everything, None)),
        check_vma=False,
    )

    def whole(object_real, object_imag, probe_real, probe_imag, patterns, offsets, counts):
        tables = jnp.asarray(block_tables(probe_real.shape[0]))
        return run(
            tables, object_real, object_imag, probe_real, probe_imag, patterns, offsets, counts
        )

    return whole
```

```python
import functools
import math

import jax
import jax.numpy as jnp
import numpy as np
from jax import lax
from jax.experimental import pallas as pl
from jax.experimental.pallas import tpu as pltpu
from jax.sharding import Mesh
from jax.sharding import PartitionSpec as P

FRESNEL = 12.0
GROUP = 6
PROP, DFT = 0, 2
POS = ("z", "yl", "core")


def block_tables(width):
    index = np.arange(width)
    turns = index[:, None] * index[None, :] % width
    dft = np.exp(-2j * np.pi * turns / width) / np.sqrt(width)
    freq = np.fft.fftfreq(width)
    phase = np.exp(-1j * np.pi * FRESNEL * freq * freq)
    prop = np.conj(dft) @ (phase[:, None] * dft)
    pieces = []
    for matrix in (prop, dft):
        right = np.block([[matrix.real, matrix.imag], [-matrix.imag, matrix.real]])
        for table in (right, right.T):
            high = table.astype(np.float32).astype(jnp.bfloat16)
            low = (table - high.astype(np.float64)).astype(np.float32).astype(jnp.bfloat16)
            pieces.append(np.stack([high, low]))
    return np.stack(pieces)


def split(value):
    high = value.astype(jnp.bfloat16)
    low = (value - high.astype(jnp.float32)).astype(jnp.bfloat16)
    return high, low


def dot(first, second):
    return jnp.dot(first, second, preferred_element_type=jnp.float32)


def pairs(product, table_ref, which, real, imag):
    out_real, out_imag = [], []
    for k in range(0, len(real), 2):
        found = product(table_ref, which, real[k : k + 2], imag[k : k + 2])
        out_real += found[0]
        out_imag += found[1]
    return out_real, out_imag


def left(table_ref, which, real, imag):
    field = jnp.concatenate(
        [jnp.concatenate(real, axis=1), jnp.concatenate(imag, axis=1)], axis=0
    )
    high, low = split(field)
    table_high, table_low = table_ref[which, 0], table_ref[which, 1]
    out = dot(table_high, high) + dot(table_low, high) + dot(table_high, low)
    w = real[0].shape[0]
    spans = [slice(k * w, (k + 1) * w) for k in range(len(real))]
    return [out[:w, s] for s in spans], [out[w:, s] for s in spans]


def right(table_ref, which, real, imag):
    field = jnp.concatenate(
        [jnp.concatenate([r, i], axis=1) for r, i in zip(real, imag)], axis=0
    )
    high, low = split(field)
    table_high, table_low = table_ref[which, 0], table_ref[which, 1]
    out = dot(high, table_high) + dot(high, table_low) + dot(low, table_high)
    w = real[0].shape[0]
    spans = [slice(k * w, (k + 1) * w) for k in range(len(real))]
    return [out[s, :w] for s in spans], [out[s, w:] for s in spans]


def transform(table_ref, base, adjoint, field):
    flip = 1 if adjoint else 0
    field = pairs(left, table_ref, base + 1 - flip, *field)
    return pairs(right, table_ref, base + flip, *field)


def mul(first, second):
    real = [p * r - q * s for p, q, r, s in zip(*first, *second)]
    imag = [p * s + q * r for p, q, r, s in zip(*first, *second)]
    return real, imag


def conj_mul(first, second):
    real = [p * r + q * s for p, q, r, s in zip(*first, *second)]
    imag = [p * s - q * r for p, q, r, s in zip(*first, *second)]
    return real, imag


def slots_kernel(
    scale,
    place_ref,
    off_ref,
    cnt_ref,
    probe_real_ref,
    probe_imag_ref,
    pat_ref,
    tab_ref,
    near_ref,
    far_ref,
    keep_ref,
    send_ref,
    obj_ref,
    grad_ref,
):
    w = probe_real_ref.shape[0]
    slots = pat_ref.shape[0]
    slices = obj_ref.shape[1]
    half = 4
    yl = place_ref[0]
    first_core = place_ref[1] == 0
    grad_ref[...] = jnp.zeros_like(grad_ref)
    top = lax.broadcasted_iota(jnp.int32, (2 * half, w), 0) < half

    def eight_rows(y, z):
        return pl.ds(pl.multiple_of((2 * z + lax.rem(y + yl, 2)) * 2 * half, 2 * half), 2 * half)

    def unpack(z, _):
        for y in range(2):
            rows = eight_rows(y, z)
            near = near_ref[y, z].astype(jnp.float32)
            far = far_ref[y, z].astype(jnp.float32)
            low = jnp.where(first_core, near, far)
            high = jnp.where(first_core, far, near)
            for s in range(slices):
                for h in range(2):
                    k = (s * 2 + h) * 2 * half
                    a, b = low[k : k + 2 * half], high[k : k + 2 * half]
                    obj_ref[0, s, h, rows, :] = jnp.where(top, a, pltpu.roll(b, half, 0))
                    obj_ref[1, s, h, rows, :] = jnp.where(top, pltpu.roll(a, half, 0), b)
        return 0

    def pack(z, _):
        for y in range(2):
            rows = eight_rows(y, z)
            for s in range(slices):
                for h in range(2):
                    k = (s * 2 + h) * 2 * half
                    real = grad_ref[0, s, h, rows, :]
                    imag = grad_ref[1, s, h, rows, :]
                    low = jnp.where(top, real, pltpu.roll(imag, half, 0))
                    high = jnp.where(top, pltpu.roll(real, half, 0), imag)
                    keep_ref[y, z, k : k + 2 * half] = jnp.where(first_core, low, high)
                    send_ref[y, z, k : k + 2 * half] = jnp.where(first_core, high, low)
        return 0

    blocks = near_ref.shape[1]
    lax.fori_loop(0, blocks, unpack, 0)

    count = cnt_ref[0, 0]
    lane = lax.broadcasted_iota(jnp.int32, (w, w), 1)

    def visit(step, _):
        numbers = [jnp.minimum(step * GROUP + k, slots - 1) for k in range(GROUP)]
        rows = [off_ref[0, n, 0] for n in numbers]
        cols = [off_ref[0, n, 1] for n in numbers]
        weights = [
            jnp.where(step * GROUP + k < count, scale, 0.0).astype(jnp.float32)
            for k in range(GROUP)
        ]
        turn = [lax.rem(c, w) for c in cols]
        back_turn = [lax.rem(2 * w - c, w) for c in cols]

        def window(part, layer):
            found = []
            for k in range(GROUP):
                near = obj_ref[part, layer, 0, pl.ds(rows[k], w), :]
                after = obj_ref[part, layer, 1, pl.ds(rows[k], w), :]
                found.append(pltpu.roll(jnp.where(lane >= cols[k], near, after), back_turn[k], 1))
            return found

        layers = [(window(0, s), window(1, s)) for s in range(slices)]
        wave = ([probe_real_ref[...]] * GROUP, [probe_imag_ref[...]] * GROUP)
        waves = []
        for s in range(slices):
            waves.append(wave)
            leaving = mul(wave, layers[s])
            if s < slices - 1:
                wave = transform(tab_ref, PROP, False, leaving)
        far = transform(tab_ref, DFT, False, leaving)
        misfit = [
            r * r + i * i - pat_ref[n].astype(jnp.float32) for r, i, n in zip(*far, numbers)
        ]
        back = ([m * r for m, r in zip(misfit, far[0])], [m * i for m, i in zip(misfit, far[1])])
        back = transform(tab_ref, DFT, True, back)
        for s in range(slices - 1, -1, -1):
            term = conj_mul(waves[s], back)
            for part in range(2):
                for k in range(GROUP):
                    moved = pltpu.roll(term[part][k] * weights[k], turn[k], 1)
                    here = lane >= cols[k]
                    grad_ref[part, s, 0, pl.ds(rows[k], w), :] += jnp.where(here, moved, 0.0)
                    grad_ref[part, s, 1, pl.ds(rows[k], w), :] += jnp.where(here, 0.0, moved)
            if s > 0:
                back = transform(tab_ref, PROP, True, conj_mul(layers[s], back))
        return 0

    lax.fori_loop(0, lax.div(count + (GROUP - 1), GROUP), visit, 0)
    lax.fori_loop(0, blocks, pack, 0)


def slots_call(scale, place, offsets, counts, probe, patterns, tables, near, far):
    slices = 3
    width = probe[0].shape[0]
    vector = pl.BlockSpec(memory_space=pltpu.VMEM)
    scalar = pl.BlockSpec(memory_space=pltpu.SMEM)
    held = pltpu.VMEM((2, slices, 2, near.shape[1] * 16, width), jnp.float32)
    return pl.pallas_call(
        functools.partial(slots_kernel, scale),
        out_shape=[jax.ShapeDtypeStruct(near.shape, jnp.float32)] * 2,
        in_specs=[scalar] * 3 + [vector] * 6,
        out_specs=[vector] * 2,
        scratch_shapes=[held, held],
        compiler_params=pltpu.CompilerParams(vmem_limit_bytes=44 * 1024 * 1024),
        name="slots",
    )(place, offsets, counts, *probe, patterns, tables, near, far)


def swap(block, axis):
    return lax.ppermute(block, axis, [(0, 1), (1, 0)])


def shift(block, distance):
    bands = lax.axis_size("region")
    return lax.ppermute(block, "region", [(i, (i + distance) % bands) for i in range(bands)])


def shift_and_swap(block, distance):
    bands = lax.axis_size("region")
    route = [(2 * i + y, (i + distance) % bands * 2 + 1 - y) for i in range(bands) for y in (0, 1)]
    return lax.ppermute(block, ("region", "yl"), route)


def encode(blocks, over):
    most = jnp.max(jnp.abs(blocks), axis=over, keepdims=True)
    code = jnp.ceil(jnp.log2(jnp.maximum(most, 1e-37)) * 64.0)
    share = jnp.clip(jnp.round(blocks * jnp.exp2(code / -64.0) * 32767.0), -32767.0, 32767.0)
    return share.astype(jnp.int16), code[0].astype(jnp.int16)


def decode(message, axis):
    code = lax.slice_in_dim(message, message.shape[axis] - 1, None, axis=axis)
    share = lax.slice_in_dim(message, 0, message.shape[axis] - 1, axis=axis)
    return share.astype(jnp.float32) * (jnp.exp2(code.astype(jnp.float32) / 64.0) / 32767.0)


def local(tables, object_real, object_imag, probe_real, probe_imag, patterns, offsets, counts):
    slices, rows, columns = object_real.shape
    width = probe_real.shape[0]
    halves = columns // width
    depth = lax.axis_size("z")
    below = width // (4 * rows)
    packed = slices * halves * 2 * rows
    place = jnp.stack([lax.axis_index("yl"), lax.axis_index("core")]).astype(jnp.int32)
    scale = 1.0 / math.sqrt(patterns.shape[1] * depth * 4)

    with jax.named_scope("gather"):
        block = jnp.stack([object_real, object_imag]).reshape(2, slices, rows, halves, width)
        block = block.transpose(1, 3, 0, 2, 4).reshape(packed, width)
        column = lax.all_to_all(
            jnp.broadcast_to(block, (depth, packed, width)), "z", 0, 0, tiled=True
        )
        other = swap(column, "yl")
        following_other = shift_and_swap(column[:below], -1)
        following = swap(following_other, "yl")
        near = jnp.concatenate([column, following, other, following_other])
        near = near.reshape(2, depth + below, packed, width)
        far = swap(near, "core")

    keep, send = slots_call(
        scale, place, offsets, counts, (probe_real, probe_imag), patterns[0], tables, near, far
    )

    with jax.named_scope("reduce"):
        total = keep + swap(send, "core")
        away = jnp.concatenate([total[1], total[0, depth:]])
        share, code = encode(away, (0,))
        code = code[None]
        near_next = jnp.concatenate([share[depth + below :], code])
        far_next = jnp.concatenate([share[depth : depth + below], code])
        beside = jnp.concatenate([share[:depth], code])
        far_next = shift_and_swap(far_next, 1)
        near_next = shift(near_next, 1)
        beside = swap(beside, "yl")
        total = total[0, :depth] + decode(beside, 0)
        total = total.at[:below].add(decode(near_next, 0) + decode(far_next, 0))
        total = total.reshape(depth, -1, 2 * rows, width)
        share, code = encode(total, (0, 1))
        code = jnp.broadcast_to(code, (depth,) + code.shape)
        message = jnp.concatenate([share, code], axis=1).reshape(depth, -1, width)
        message = lax.all_to_all(message, "z", 0, 0, tiled=True)
        total = decode(message.reshape(depth, -1, 2 * rows, width), 1).sum(0)
        total = total.reshape(slices, halves, 2, rows, width).transpose(2, 0, 3, 1, 4)
        total = total.reshape(2, slices, rows, columns)
    return total[0], total[1]


def solution(mesh):
    fine = Mesh(mesh.devices.reshape(mesh.shape["region"], -1, 2, 2), ("region",) + POS)
    everything = ("region",) + POS
    run = jax.shard_map(
        local,
        mesh=fine,
        in_specs=(
            P(),
            P(None, everything, None),
            P(None, everything, None),
            P(),
            P(),
            P("region", POS, None, None),
            P("region", POS, None),
            P("region", POS),
        ),
        out_specs=(P(None, everything, None), P(None, everything, None)),
        check_vma=False,
    )

    def whole(object_real, object_imag, probe_real, probe_imag, patterns, offsets, counts):
        tables = jnp.asarray(block_tables(probe_real.shape[0]))
        return run(
            tables, object_real, object_imag, probe_real, probe_imag, patterns, offsets, counts
        )

    return whole
```

```python
import functools
import math

import jax
import jax.numpy as jnp
import numpy as np
from jax import lax
from jax.experimental import pallas as pl
from jax.experimental.pallas import tpu as pltpu
from jax.sharding import Mesh
from jax.sharding import PartitionSpec as P

FRESNEL = 12.0
GROUP = 6
PROP, DFT = 0, 2
POS = ("z", "yl", "core")


def block_tables(width):
    index = np.arange(width)
    turns = index[:, None] * index[None, :] % width
    dft = np.exp(-2j * np.pi * turns / width) / np.sqrt(width)
    freq = np.fft.fftfreq(width)
    phase = np.exp(-1j * np.pi * FRESNEL * freq * freq)
    prop = np.conj(dft) @ (phase[:, None] * dft)
    pieces = []
    for matrix in (prop, dft):
        right = np.block([[matrix.real, matrix.imag], [-matrix.imag, matrix.real]])
        for table in (right, right.T):
            high = table.astype(np.float32).astype(jnp.bfloat16)
            low = (table - high.astype(np.float64)).astype(np.float32).astype(jnp.bfloat16)
            pieces.append(np.stack([high, low]))
    return np.stack(pieces)


def split(value):
    high = value.astype(jnp.bfloat16)
    low = (value - high.astype(jnp.float32)).astype(jnp.bfloat16)
    return high, low


def dot(first, second):
    return jnp.dot(first, second, preferred_element_type=jnp.float32)


def pairs(product, table_ref, which, real, imag):
    out_real, out_imag = [], []
    for k in range(0, len(real), 2):
        found = product(table_ref, which, real[k : k + 2], imag[k : k + 2])
        out_real += found[0]
        out_imag += found[1]
    return out_real, out_imag


def left(table_ref, which, real, imag):
    field = jnp.concatenate(
        [jnp.concatenate(real, axis=1), jnp.concatenate(imag, axis=1)], axis=0
    )
    high, low = split(field)
    table_high, table_low = table_ref[which, 0], table_ref[which, 1]
    out = dot(table_high, high) + dot(table_low, high) + dot(table_high, low)
    w = real[0].shape[0]
    spans = [slice(k * w, (k + 1) * w) for k in range(len(real))]
    return [out[:w, s] for s in spans], [out[w:, s] for s in spans]


def right(table_ref, which, real, imag):
    field = jnp.concatenate(
        [jnp.concatenate([r, i], axis=1) for r, i in zip(real, imag)], axis=0
    )
    high, low = split(field)
    table_high, table_low = table_ref[which, 0], table_ref[which, 1]
    out = dot(high, table_high) + dot(high, table_low) + dot(low, table_high)
    w = real[0].shape[0]
    spans = [slice(k * w, (k + 1) * w) for k in range(len(real))]
    return [out[s, :w] for s in spans], [out[s, w:] for s in spans]


def transform(table_ref, base, adjoint, field):
    flip = 1 if adjoint else 0
    field = pairs(left, table_ref, base + 1 - flip, *field)
    return pairs(right, table_ref, base + flip, *field)


def mul(first, second):
    real = [p * r - q * s for p, q, r, s in zip(*first, *second)]
    imag = [p * s + q * r for p, q, r, s in zip(*first, *second)]
    return real, imag


def conj_mul(first, second):
    real = [p * r + q * s for p, q, r, s in zip(*first, *second)]
    imag = [p * s - q * r for p, q, r, s in zip(*first, *second)]
    return real, imag


def slots_kernel(
    scale,
    place_ref,
    off_ref,
    cnt_ref,
    probe_real_ref,
    probe_imag_ref,
    pat_ref,
    tab_ref,
    own_ref,
    next_ref,
    keep_ref,
    send_ref,
    obj_ref,
    grad_ref,
):
    w = probe_real_ref.shape[0]
    slots = pat_ref.shape[0]
    slices = obj_ref.shape[1]
    half = 4
    yl = place_ref[0]
    first_core = place_ref[1] == 0
    grad_ref[...] = jnp.zeros_like(grad_ref)
    top = lax.broadcasted_iota(jnp.int32, (2 * half, w), 0) < half

    def eight_rows(y, z):
        return pl.ds(pl.multiple_of((2 * z + lax.rem(y + yl, 2)) * 2 * half, 2 * half), 2 * half)

    def place(low, high, rows):
        low, high = low.astype(jnp.float32), high.astype(jnp.float32)
        for s in range(slices):
            for h in range(2):
                k = (s * 2 + h) * 2 * half
                a, b = low[k : k + 2 * half], high[k : k + 2 * half]
                obj_ref[0, s, h, rows, :] = jnp.where(top, a, pltpu.roll(b, half, 0))
                obj_ref[1, s, h, rows, :] = jnp.where(top, pltpu.roll(a, half, 0), b)

    def unpack_own(z, _):
        for y in range(2):
            row = pl.multiple_of((2 * z + y) * 2 * half, 2 * half)
            place(own_ref[2 * y, z], own_ref[2 * y + 1, z], pl.ds(row, 2 * half))
        return 0

    def unpack_next(z, _):
        for y in range(2):
            place(next_ref[0, y, z], next_ref[1, y, z], eight_rows(y, z + own_ref.shape[1]))
        return 0

    def pack(z, _):
        for y in range(2):
            rows = eight_rows(y, z)
            for s in range(slices):
                for h in range(2):
                    k = (s * 2 + h) * 2 * half
                    real = grad_ref[0, s, h, rows, :]
                    imag = grad_ref[1, s, h, rows, :]
                    low = jnp.where(top, real, pltpu.roll(imag, half, 0))
                    high = jnp.where(top, pltpu.roll(real, half, 0), imag)
                    keep_ref[y, z, k : k + 2 * half] = jnp.where(first_core, low, high)
                    send_ref[y, z, k : k + 2 * half] = jnp.where(first_core, high, low)
        return 0

    lax.fori_loop(0, own_ref.shape[1], unpack_own, 0)
    lax.fori_loop(0, next_ref.shape[2], unpack_next, 0)

    count = cnt_ref[0, 0]
    lane = lax.broadcasted_iota(jnp.int32, (w, w), 1)

    def visit(step, _):
        numbers = [jnp.minimum(step * GROUP + k, slots - 1) for k in range(GROUP)]
        rows = [off_ref[0, n, 0] for n in numbers]
        cols = [off_ref[0, n, 1] for n in numbers]
        weights = [
            jnp.where(step * GROUP + k < count, scale, 0.0).astype(jnp.float32)
            for k in range(GROUP)
        ]
        turn = [lax.rem(c, w) for c in cols]
        back_turn = [lax.rem(2 * w - c, w) for c in cols]

        def window(part, layer):
            found = []
            for k in range(GROUP):
                near = obj_ref[part, layer, 0, pl.ds(rows[k], w), :]
                after = obj_ref[part, layer, 1, pl.ds(rows[k], w), :]
                found.append(pltpu.roll(jnp.where(lane >= cols[k], near, after), back_turn[k], 1))
            return found

        layers = [(window(0, s), window(1, s)) for s in range(slices)]
        wave = ([probe_real_ref[...]] * GROUP, [probe_imag_ref[...]] * GROUP)
        waves = []
        for s in range(slices):
            waves.append(wave)
            leaving = mul(wave, layers[s])
            if s < slices - 1:
                wave = transform(tab_ref, PROP, False, leaving)
        far = transform(tab_ref, DFT, False, leaving)
        misfit = [
            (r * r + i * i - pat_ref[n].astype(jnp.float32)) * weight
            for r, i, n, weight in zip(*far, numbers, weights)
        ]
        back = ([m * r for m, r in zip(misfit, far[0])], [m * i for m, i in zip(misfit, far[1])])
        back = transform(tab_ref, DFT, True, back)
        for s in range(slices - 1, -1, -1):
            term = conj_mul(waves[s], back)
            for part in range(2):
                for k in range(GROUP):
                    moved = pltpu.roll(term[part][k], turn[k], 1)
                    here = lane >= cols[k]
                    grad_ref[part, s, 0, pl.ds(rows[k], w), :] += jnp.where(here, moved, 0.0)
                    grad_ref[part, s, 1, pl.ds(rows[k], w), :] += jnp.where(here, 0.0, moved)
            if s > 0:
                back = transform(tab_ref, PROP, True, conj_mul(layers[s], back))
        return 0

    lax.fori_loop(0, lax.div(count + (GROUP - 1), GROUP), visit, 0)
    lax.fori_loop(0, keep_ref.shape[1], pack, 0)


def slots_call(scale, place, offsets, counts, probe, patterns, tables, own, following):
    slices = 3
    width = probe[0].shape[0]
    vector = pl.BlockSpec(memory_space=pltpu.VMEM)
    scalar = pl.BlockSpec(memory_space=pltpu.SMEM)
    blocks = own.shape[1] + following.shape[2]
    held = pltpu.VMEM((2, slices, 2, blocks * 16, width), jnp.float32)
    out = jax.ShapeDtypeStruct((2, blocks) + own.shape[2:], jnp.float32)
    return pl.pallas_call(
        functools.partial(slots_kernel, scale),
        out_shape=[out] * 2,
        in_specs=[scalar] * 3 + [vector] * 6,
        out_specs=[vector] * 2,
        scratch_shapes=[held, held],
        compiler_params=pltpu.CompilerParams(vmem_limit_bytes=44 * 1024 * 1024),
        name="slots",
    )(place, offsets, counts, *probe, patterns, tables, own, following)


def swap(block, axis):
    return lax.ppermute(block, axis, [(0, 1), (1, 0)])


def shift(block, distance):
    bands = lax.axis_size("region")
    return lax.ppermute(block, "region", [(i, (i + distance) % bands) for i in range(bands)])


def shift_and_swap(block, distance):
    bands = lax.axis_size("region")
    route = [(2 * i + y, (i + distance) % bands * 2 + 1 - y) for i in range(bands) for y in (0, 1)]
    return lax.ppermute(block, ("region", "yl"), route)


def encode(blocks):
    most = jnp.max(jnp.abs(blocks), axis=(0, 1), keepdims=True)
    code = jnp.ceil(jnp.log2(jnp.maximum(most, 1e-37)) * 64.0)
    share = jnp.clip(jnp.round(blocks * jnp.exp2(code / -64.0) * 32767.0), -32767.0, 32767.0)
    return share.astype(jnp.int16), code[0].astype(jnp.int16)


def decode(share, code):
    return share.astype(jnp.float32) * (jnp.exp2(code.astype(jnp.float32) / 64.0) / 32767.0)


def carry(send, share, code):
    tile = code.shape[-2:]
    moved = send(jnp.concatenate([share.reshape(-1, *tile), code]))
    return decode(moved[:-1], moved[-1]).reshape(share.shape)


def local(tables, object_real, object_imag, probe_real, probe_imag, patterns, offsets, counts):
    slices, rows, columns = object_real.shape
    width = probe_real.shape[0]
    halves = columns // width
    depth = lax.axis_size("z")
    below = width // (4 * rows)
    packed = slices * halves * 2 * rows
    place = jnp.stack([lax.axis_index("yl"), lax.axis_index("core")]).astype(jnp.int32)
    scale = 1.0 / math.sqrt(patterns.shape[1] * depth * 4)

    with jax.named_scope("gather"):
        block = jnp.stack([object_real, object_imag]).reshape(2, slices, rows, halves, width)
        block = block.transpose(1, 3, 0, 2, 4).reshape(packed, width)
        column = lax.all_to_all(
            jnp.broadcast_to(block, (depth, packed, width)), "z", 0, 0, tiled=True
        )
        column, offsets, place = lax.optimization_barrier((column, offsets, place))
        following = jnp.stack([shift(column[:below], -1), shift_and_swap(column[:below], -1)])
        own = lax.all_gather(column, ("yl", "core"), axis=0)
        following = lax.all_gather(following, "core", axis=0)

    keep, send = slots_call(
        scale, place, offsets, counts, (probe_real, probe_imag), patterns[0], tables, own, following
    )

    with jax.named_scope("reduce"):
        total = keep + swap(send, "core")
        total = total.reshape(2, depth + below, -1, 2 * rows, width)
        away = jnp.concatenate([total[1], total[0, depth:]])
        share, code = encode(away)
        near_next = carry(lambda x: shift(x, 1), share[depth + below :], code)
        far_next = carry(lambda x: shift_and_swap(x, 1), share[depth : depth + below], code)
        beside = carry(lambda x: swap(x, "yl"), share[:depth], code)
        total = (total[0, :depth] + beside).at[:below].add(near_next + far_next)
        share, code = encode(total)
        code = jnp.broadcast_to(code, (depth,) + code.shape)
        parts = jnp.concatenate([share, code], axis=1).reshape(depth, -1, width)
        parts = lax.all_to_all(parts, "z", 0, 0, tiled=True)
        parts = parts.reshape(depth, -1, 2 * rows, width)
        total = decode(parts[:, :-1], parts[:, -1:]).sum(0)
        total = total.reshape(slices, halves, 2, rows, width).transpose(2, 0, 3, 1, 4)
        total = total.reshape(2, slices, rows, columns)
    return total[0], total[1]


def solution(mesh):
    fine = Mesh(mesh.devices.reshape(mesh.shape["region"], -1, 2, 2), ("region",) + POS)
    everything = ("region",) + POS
    run = jax.shard_map(
        local,
        mesh=fine,
        in_specs=(
            P(),
            P(None, everything, None),
            P(None, everything, None),
            P(),
            P(),
            P("region", POS, None, None),
            P("region", POS, None),
            P("region", POS),
        ),
        out_specs=(P(None, everything, None), P(None, everything, None)),
        check_vma=False,
    )

    def whole(object_real, object_imag, probe_real, probe_imag, patterns, offsets, counts):
        tables = jnp.asarray(block_tables(probe_real.shape[0]))
        return run(
            tables, object_real, object_imag, probe_real, probe_imag, patterns, offsets, counts
        )

    return whole
```

```python
import functools
import math

import jax
import jax.numpy as jnp
import numpy as np
from jax import lax
from jax.experimental import pallas as pl
from jax.experimental.pallas import tpu as pltpu
from jax.sharding import Mesh
from jax.sharding import PartitionSpec as P

FRESNEL = 12.0
GROUP = 6
PROP, DFT = 0, 2
POS = ("z", "yl", "core")


def block_tables(width):
    index = np.arange(width)
    turns = index[:, None] * index[None, :] % width
    dft = np.exp(-2j * np.pi * turns / width) / np.sqrt(width)
    freq = np.fft.fftfreq(width)
    phase = np.exp(-1j * np.pi * FRESNEL * freq * freq)
    prop = np.conj(dft) @ (phase[:, None] * dft)
    pieces = []
    for matrix in (prop, dft):
        right = np.block([[matrix.real, matrix.imag], [-matrix.imag, matrix.real]])
        for table in (right, right.T):
            high = table.astype(np.float32).astype(jnp.bfloat16)
            low = (table - high.astype(np.float64)).astype(np.float32).astype(jnp.bfloat16)
            pieces.append(np.stack([high, low]))
    return np.stack(pieces)


def split(value):
    high = value.astype(jnp.bfloat16)
    low = (value - high.astype(jnp.float32)).astype(jnp.bfloat16)
    return high, low


def dot(first, second):
    return jnp.dot(first, second, preferred_element_type=jnp.float32)


def pairs(product, table_ref, which, real, imag):
    out_real, out_imag = [], []
    for k in range(0, len(real), 2):
        found = product(table_ref, which, real[k : k + 2], imag[k : k + 2])
        out_real += found[0]
        out_imag += found[1]
    return out_real, out_imag


def left(table_ref, which, real, imag):
    field = jnp.concatenate(
        [jnp.concatenate(real, axis=1), jnp.concatenate(imag, axis=1)], axis=0
    )
    high, low = split(field)
    table_high, table_low = table_ref[which, 0], table_ref[which, 1]
    out = dot(table_high, high) + dot(table_low, high) + dot(table_high, low)
    w = real[0].shape[0]
    spans = [slice(k * w, (k + 1) * w) for k in range(len(real))]
    return [out[:w, s] for s in spans], [out[w:, s] for s in spans]


def right(table_ref, which, real, imag):
    field = jnp.concatenate(
        [jnp.concatenate([r, i], axis=1) for r, i in zip(real, imag)], axis=0
    )
    high, low = split(field)
    table_high, table_low = table_ref[which, 0], table_ref[which, 1]
    out = dot(high, table_high) + dot(high, table_low) + dot(low, table_high)
    w = real[0].shape[0]
    spans = [slice(k * w, (k + 1) * w) for k in range(len(real))]
    return [out[s, :w] for s in spans], [out[s, w:] for s in spans]


def transform(table_ref, base, adjoint, field):
    flip = 1 if adjoint else 0
    field = pairs(left, table_ref, base + 1 - flip, *field)
    return pairs(right, table_ref, base + flip, *field)


def mul(first, second):
    real = [p * r - q * s for p, q, r, s in zip(*first, *second)]
    imag = [p * s + q * r for p, q, r, s in zip(*first, *second)]
    return real, imag


def conj_mul(first, second):
    real = [p * r + q * s for p, q, r, s in zip(*first, *second)]
    imag = [p * s - q * r for p, q, r, s in zip(*first, *second)]
    return real, imag


def slots_kernel(
    scale,
    place_ref,
    off_ref,
    cnt_ref,
    probe_real_ref,
    probe_imag_ref,
    pat_ref,
    tab_ref,
    own_ref,
    next_ref,
    keep_ref,
    send_ref,
    obj_ref,
    grad_ref,
):
    w = probe_real_ref.shape[0]
    slots = pat_ref.shape[0]
    slices = obj_ref.shape[1]
    half = 4
    yl = place_ref[0]
    first_core = place_ref[1] == 0
    grad_ref[...] = jnp.zeros_like(grad_ref)
    top = lax.broadcasted_iota(jnp.int32, (2 * half, w), 0) < half

    def eight_rows(y, z):
        return pl.ds(pl.multiple_of((2 * z + lax.rem(y + yl, 2)) * 2 * half, 2 * half), 2 * half)

    def place(low, high, rows):
        low, high = low.astype(jnp.float32), high.astype(jnp.float32)
        for s in range(slices):
            for h in range(2):
                k = (s * 2 + h) * 2 * half
                a, b = low[k : k + 2 * half], high[k : k + 2 * half]
                obj_ref[0, s, h, rows, :] = jnp.where(top, a, pltpu.roll(b, half, 0))
                obj_ref[1, s, h, rows, :] = jnp.where(top, pltpu.roll(a, half, 0), b)

    def unpack_own(z, _):
        for y in range(2):
            row = pl.multiple_of((2 * z + y) * 2 * half, 2 * half)
            place(own_ref[2 * y, z], own_ref[2 * y + 1, z], pl.ds(row, 2 * half))
        return 0

    def unpack_next(z, _):
        for y in range(2):
            place(next_ref[0, y, z], next_ref[1, y, z], eight_rows(y, z + own_ref.shape[1]))
        return 0

    def pack(z, _):
        for y in range(2):
            rows = eight_rows(y, z)
            for s in range(slices):
                for h in range(2):
                    k = (s * 2 + h) * 2 * half
                    real = grad_ref[0, s, h, rows, :]
                    imag = grad_ref[1, s, h, rows, :]
                    low = jnp.where(top, real, pltpu.roll(imag, half, 0))
                    high = jnp.where(top, pltpu.roll(real, half, 0), imag)
                    keep_ref[y, z, k : k + 2 * half] = jnp.where(first_core, low, high)
                    send_ref[y, z, k : k + 2 * half] = jnp.where(first_core, high, low)
        return 0

    lax.fori_loop(0, own_ref.shape[1], unpack_own, 0, unroll=4)
    lax.fori_loop(0, next_ref.shape[2], unpack_next, 0, unroll=4)

    count = cnt_ref[0, 0]
    lane = lax.broadcasted_iota(jnp.int32, (w, w), 1)

    def visit(step, _):
        numbers = [jnp.minimum(step * GROUP + k, slots - 1) for k in range(GROUP)]
        rows = [off_ref[0, n, 0] for n in numbers]
        cols = [off_ref[0, n, 1] for n in numbers]
        weights = [
            jnp.where(step * GROUP + k < count, scale, 0.0).astype(jnp.float32)
            for k in range(GROUP)
        ]
        turn = [lax.rem(c, w) for c in cols]
        back_turn = [lax.rem(2 * w - c, w) for c in cols]

        def window(part, layer):
            found = []
            for k in range(GROUP):
                near = obj_ref[part, layer, 0, pl.ds(rows[k], w), :]
                after = obj_ref[part, layer, 1, pl.ds(rows[k], w), :]
                found.append(pltpu.roll(jnp.where(lane >= cols[k], near, after), back_turn[k], 1))
            return found

        layers = [(window(0, s), window(1, s)) for s in range(slices)]
        wave = ([probe_real_ref[...]] * GROUP, [probe_imag_ref[...]] * GROUP)
        waves = []
        for s in range(slices):
            waves.append(wave)
            leaving = mul(wave, layers[s])
            if s < slices - 1:
                wave = transform(tab_ref, PROP, False, leaving)
        far = transform(tab_ref, DFT, False, leaving)
        misfit = [
            (r * r + i * i - pat_ref[n].astype(jnp.float32)) * weight
            for r, i, n, weight in zip(*far, numbers, weights)
        ]
        back = ([m * r for m, r in zip(misfit, far[0])], [m * i for m, i in zip(misfit, far[1])])
        back = transform(tab_ref, DFT, True, back)
        for s in range(slices - 1, -1, -1):
            term = conj_mul(waves[s], back)
            for part in range(2):
                for k in range(GROUP):
                    moved = pltpu.roll(term[part][k], turn[k], 1)
                    here = lane >= cols[k]
                    grad_ref[part, s, 0, pl.ds(rows[k], w), :] += jnp.where(here, moved, 0.0)
                    grad_ref[part, s, 1, pl.ds(rows[k], w), :] += jnp.where(here, 0.0, moved)
            if s > 0:
                back = transform(tab_ref, PROP, True, conj_mul(layers[s], back))
        return 0

    lax.fori_loop(0, lax.div(count + (GROUP - 1), GROUP), visit, 0)
    lax.fori_loop(0, keep_ref.shape[1], pack, 0, unroll=4)


def slots_call(scale, place, offsets, counts, probe, patterns, tables, own, following):
    slices = 3
    width = probe[0].shape[0]
    vector = pl.BlockSpec(memory_space=pltpu.VMEM)
    scalar = pl.BlockSpec(memory_space=pltpu.SMEM)
    blocks = own.shape[1] + following.shape[2]
    held = pltpu.VMEM((2, slices, 2, blocks * 16, width), jnp.float32)
    out = jax.ShapeDtypeStruct((2, blocks) + own.shape[2:], jnp.float32)
    return pl.pallas_call(
        functools.partial(slots_kernel, scale),
        out_shape=[out] * 2,
        in_specs=[scalar] * 3 + [vector] * 6,
        out_specs=[vector] * 2,
        scratch_shapes=[held, held],
        compiler_params=pltpu.CompilerParams(vmem_limit_bytes=44 * 1024 * 1024),
        name="slots",
    )(place, offsets, counts, *probe, patterns, tables, own, following)


def swap(block, axis):
    return lax.ppermute(block, axis, [(0, 1), (1, 0)])


def shift(block, distance):
    bands = lax.axis_size("region")
    return lax.ppermute(block, "region", [(i, (i + distance) % bands) for i in range(bands)])


def shift_and_swap(block, distance):
    bands = lax.axis_size("region")
    route = [(2 * i + y, (i + distance) % bands * 2 + 1 - y) for i in range(bands) for y in (0, 1)]
    return lax.ppermute(block, ("region", "yl"), route)


def encode(blocks):
    most = jnp.max(jnp.abs(blocks), axis=(0, 1), keepdims=True)
    code = jnp.ceil(jnp.log2(jnp.maximum(most, 1e-37)) * 64.0)
    share = jnp.clip(jnp.round(blocks * jnp.exp2(code / -64.0) * 32767.0), -32767.0, 32767.0)
    return share.astype(jnp.int16), code[0].astype(jnp.int16)


def decode(share, code):
    return share.astype(jnp.float32) * (jnp.exp2(code.astype(jnp.float32) / 64.0) / 32767.0)


def carry(send, share, code):
    tile = code.shape[-2:]
    moved = send(jnp.concatenate([share.reshape(-1, *tile), code]))
    return decode(moved[:-1], moved[-1]).reshape(share.shape)


def local(tables, object_real, object_imag, probe_real, probe_imag, patterns, offsets, counts):
    slices, rows, columns = object_real.shape
    width = probe_real.shape[0]
    halves = columns // width
    depth = lax.axis_size("z")
    below = width // (4 * rows)
    packed = slices * halves * 2 * rows
    place = jnp.stack([lax.axis_index("yl"), lax.axis_index("core")]).astype(jnp.int32)
    scale = 1.0 / math.sqrt(patterns.shape[1] * depth * 4)

    with jax.named_scope("gather"):
        block = jnp.stack([object_real, object_imag]).reshape(2, slices, rows, halves, width)
        block = block.transpose(1, 3, 0, 2, 4).reshape(packed, width)
        column = lax.all_to_all(
            jnp.broadcast_to(block, (depth, packed, width)), "z", 0, 0, tiled=True
        )
        column, offsets, place = lax.optimization_barrier((column, offsets, place))
        following = jnp.stack([shift(column[:below], -1), shift_and_swap(column[:below], -1)])
        own = lax.all_gather(column, ("yl", "core"), axis=0)
        following = lax.all_gather(following, "core", axis=0)

    keep, send = slots_call(
        scale, place, offsets, counts, (probe_real, probe_imag), patterns[0], tables, own, following
    )

    with jax.named_scope("reduce"):
        total = keep + swap(send, "core")
        total = total.reshape(2, depth + below, -1, 2 * rows, width)
        away = jnp.concatenate([total[1], total[0, depth:]])
        share, code = encode(away)
        near_next = carry(lambda x: shift(x, 1), share[depth + below :], code)
        far_next = carry(lambda x: shift_and_swap(x, 1), share[depth : depth + below], code)
        beside = carry(lambda x: swap(x, "yl"), share[:depth], code)
        total = (total[0, :depth] + beside).at[:below].add(near_next + far_next)
        share, code = encode(total)
        code = jnp.broadcast_to(code, (depth,) + code.shape)
        parts = jnp.concatenate([share, code], axis=1).reshape(depth, -1, width)
        parts = lax.all_to_all(parts, "z", 0, 0, tiled=True)
        parts = parts.reshape(depth, -1, 2 * rows, width)
        total = decode(parts[:, :-1], parts[:, -1:]).sum(0)
        total = total.reshape(slices, halves, 2, rows, width).transpose(2, 0, 3, 1, 4)
        total = total.reshape(2, slices, rows, columns)
    return total[0], total[1]


def solution(mesh):
    fine = Mesh(mesh.devices.reshape(mesh.shape["region"], -1, 2, 2), ("region",) + POS)
    everything = ("region",) + POS
    run = jax.shard_map(
        local,
        mesh=fine,
        in_specs=(
            P(),
            P(None, everything, None),
            P(None, everything, None),
            P(),
            P(),
            P("region", POS, None, None),
            P("region", POS, None),
            P("region", POS),
        ),
        out_specs=(P(None, everything, None), P(None, everything, None)),
        check_vma=False,
    )

    def whole(object_real, object_imag, probe_real, probe_imag, patterns, offsets, counts):
        tables = jnp.asarray(block_tables(probe_real.shape[0]))
        return run(
            tables, object_real, object_imag, probe_real, probe_imag, patterns, offsets, counts
        )

    return whole
```

```python
import functools
import math

import jax
import jax.numpy as jnp
import numpy as np
from jax import lax
from jax.experimental import pallas as pl
from jax.experimental.pallas import tpu as pltpu
from jax.sharding import Mesh
from jax.sharding import PartitionSpec as P

FRESNEL = 12.0
GROUP = 6
PROP, DFT = 0, 2
POS = ("z", "yl", "core")


def block_tables(width):
    index = np.arange(width)
    turns = index[:, None] * index[None, :] % width
    dft = np.exp(-2j * np.pi * turns / width) / np.sqrt(width)
    freq = np.fft.fftfreq(width)
    phase = np.exp(-1j * np.pi * FRESNEL * freq * freq)
    prop = np.conj(dft) @ (phase[:, None] * dft)
    pieces = []
    for matrix in (prop, dft):
        right = np.block([[matrix.real, matrix.imag], [-matrix.imag, matrix.real]])
        for table in (right, right.T):
            high = table.astype(np.float32).astype(jnp.bfloat16)
            low = (table - high.astype(np.float64)).astype(np.float32).astype(jnp.bfloat16)
            pieces.append(np.stack([high, low]))
    return np.stack(pieces)


def split(value):
    high = value.astype(jnp.bfloat16)
    low = (value - high.astype(jnp.float32)).astype(jnp.bfloat16)
    return high, low


def dot(first, second):
    return jnp.dot(first, second, preferred_element_type=jnp.float32)


def pairs(product, table_ref, which, real, imag):
    out_real, out_imag = [], []
    for k in range(0, len(real), 2):
        found = product(table_ref, which, real[k : k + 2], imag[k : k + 2])
        out_real += found[0]
        out_imag += found[1]
    return out_real, out_imag


def left(table_ref, which, real, imag):
    field = jnp.concatenate(
        [jnp.concatenate(real, axis=1), jnp.concatenate(imag, axis=1)], axis=0
    )
    high, low = split(field)
    table_high, table_low = table_ref[which, 0], table_ref[which, 1]
    out = dot(table_high, high) + dot(table_low, high) + dot(table_high, low)
    w = real[0].shape[0]
    spans = [slice(k * w, (k + 1) * w) for k in range(len(real))]
    return [out[:w, s] for s in spans], [out[w:, s] for s in spans]


def right(table_ref, which, real, imag):
    field = jnp.concatenate(
        [jnp.concatenate([r, i], axis=1) for r, i in zip(real, imag)], axis=0
    )
    high, low = split(field)
    table_high, table_low = table_ref[which, 0], table_ref[which, 1]
    out = dot(high, table_high) + dot(high, table_low) + dot(low, table_high)
    w = real[0].shape[0]
    spans = [slice(k * w, (k + 1) * w) for k in range(len(real))]
    return [out[s, :w] for s in spans], [out[s, w:] for s in spans]


def transform(table_ref, base, adjoint, field):
    flip = 1 if adjoint else 0
    field = pairs(left, table_ref, base + 1 - flip, *field)
    return pairs(right, table_ref, base + flip, *field)


def mul(first, second):
    real = [p * r - q * s for p, q, r, s in zip(*first, *second)]
    imag = [p * s + q * r for p, q, r, s in zip(*first, *second)]
    return real, imag


def conj_mul(first, second):
    real = [p * r + q * s for p, q, r, s in zip(*first, *second)]
    imag = [p * s - q * r for p, q, r, s in zip(*first, *second)]
    return real, imag


def slots_kernel(
    scale,
    place_ref,
    off_ref,
    cnt_ref,
    probe_real_ref,
    probe_imag_ref,
    pat_ref,
    tab_ref,
    own_ref,
    next_ref,
    keep_ref,
    send_ref,
    obj_ref,
    grad_ref,
):
    w = probe_real_ref.shape[0]
    slots = pat_ref.shape[0]
    slices = obj_ref.shape[1]
    half = 4
    yl = place_ref[0]
    first_core = place_ref[1] == 0
    grad_ref[...] = jnp.zeros_like(grad_ref)
    top = lax.broadcasted_iota(jnp.int32, (2 * half, w), 0) < half

    def eight_rows(y, z):
        return pl.ds(pl.multiple_of((2 * z + lax.rem(y + yl, 2)) * 2 * half, 2 * half), 2 * half)

    def place(low, high, rows):
        low, high = low.astype(jnp.float32), high.astype(jnp.float32)
        for s in range(slices):
            for h in range(2):
                k = (s * 2 + h) * 2 * half
                a, b = low[k : k + 2 * half], high[k : k + 2 * half]
                obj_ref[0, s, h, rows, :] = jnp.where(top, a, pltpu.roll(b, half, 0))
                obj_ref[1, s, h, rows, :] = jnp.where(top, pltpu.roll(a, half, 0), b)

    def unpack_own(z, _):
        for y in range(2):
            row = pl.multiple_of((2 * z + y) * 2 * half, 2 * half)
            place(own_ref[2 * y, z], own_ref[2 * y + 1, z], pl.ds(row, 2 * half))
        return 0

    def unpack_next(z, _):
        for y in range(2):
            place(next_ref[0, y, z], next_ref[1, y, z], eight_rows(y, z + own_ref.shape[1]))
        return 0

    def pack(z, _):
        for y in range(2):
            rows = eight_rows(y, z)
            for s in range(slices):
                for h in range(2):
                    k = (s * 2 + h) * 2 * half
                    real = grad_ref[0, s, h, rows, :]
                    imag = grad_ref[1, s, h, rows, :]
                    low = jnp.where(top, real, pltpu.roll(imag, half, 0))
                    high = jnp.where(top, pltpu.roll(real, half, 0), imag)
                    keep_ref[y, z, k : k + 2 * half] = jnp.where(first_core, low, high)
                    send_ref[y, z, k : k + 2 * half] = jnp.where(first_core, high, low)
        return 0

    lax.fori_loop(0, own_ref.shape[1], unpack_own, 0, unroll=4)
    lax.fori_loop(0, next_ref.shape[2], unpack_next, 0, unroll=4)

    count = cnt_ref[0, 0]
    lane = lax.broadcasted_iota(jnp.int32, (w, w), 1)

    def visit(step, _):
        numbers = [jnp.minimum(step * GROUP + k, slots - 1) for k in range(GROUP)]
        rows = [off_ref[0, n, 0] for n in numbers]
        cols = [off_ref[0, n, 1] for n in numbers]
        weights = [
            jnp.where(step * GROUP + k < count, scale, 0.0).astype(jnp.float32)
            for k in range(GROUP)
        ]
        turn = [lax.rem(c, w) for c in cols]
        back_turn = [lax.rem(2 * w - c, w) for c in cols]

        def window(part, layer):
            found = []
            for k in range(GROUP):
                near = obj_ref[part, layer, 0, pl.ds(rows[k], w), :]
                after = obj_ref[part, layer, 1, pl.ds(rows[k], w), :]
                found.append(pltpu.roll(jnp.where(lane >= cols[k], near, after), back_turn[k], 1))
            return found

        layers = [(window(0, s), window(1, s)) for s in range(slices)]
        wave = ([probe_real_ref[...]] * GROUP, [probe_imag_ref[...]] * GROUP)
        waves = []
        for s in range(slices):
            waves.append(wave)
            leaving = mul(wave, layers[s])
            if s < slices - 1:
                wave = transform(tab_ref, PROP, False, leaving)
        far = transform(tab_ref, DFT, False, leaving)
        misfit = [
            (r * r + i * i - pat_ref[n].astype(jnp.float32)) * weight
            for r, i, n, weight in zip(*far, numbers, weights)
        ]
        back = ([m * r for m, r in zip(misfit, far[0])], [m * i for m, i in zip(misfit, far[1])])
        back = transform(tab_ref, DFT, True, back)
        for s in range(slices - 1, -1, -1):
            term = conj_mul(waves[s], back)
            for part in range(2):
                for k in range(GROUP):
                    moved = pltpu.roll(term[part][k], turn[k], 1)
                    here = lane >= cols[k]
                    grad_ref[part, s, 0, pl.ds(rows[k], w), :] += jnp.where(here, moved, 0.0)
                    grad_ref[part, s, 1, pl.ds(rows[k], w), :] += jnp.where(here, 0.0, moved)
            if s > 0:
                back = transform(tab_ref, PROP, True, conj_mul(layers[s], back))
        return 0

    lax.fori_loop(0, lax.div(count + (GROUP - 1), GROUP), visit, 0)
    lax.fori_loop(0, keep_ref.shape[1], pack, 0, unroll=4)


def slots_call(scale, place, offsets, counts, probe, patterns, tables, own, following):
    slices = 3
    width = probe[0].shape[0]
    vector = pl.BlockSpec(memory_space=pltpu.VMEM)
    scalar = pl.BlockSpec(memory_space=pltpu.SMEM)
    blocks = own.shape[1] + following.shape[2]
    held = pltpu.VMEM((2, slices, 2, blocks * 16, width), jnp.float32)
    out = jax.ShapeDtypeStruct((2, blocks) + own.shape[2:], jnp.float32)
    return pl.pallas_call(
        functools.partial(slots_kernel, scale),
        out_shape=[out] * 2,
        in_specs=[scalar] * 3 + [vector] * 6,
        out_specs=[vector] * 2,
        scratch_shapes=[held, held],
        compiler_params=pltpu.CompilerParams(vmem_limit_bytes=44 * 1024 * 1024),
        name="slots",
    )(place, offsets, counts, *probe, patterns, tables, own, following)


def swap(block, axis):
    return lax.ppermute(block, axis, [(0, 1), (1, 0)])


def shift(block, distance):
    bands = lax.axis_size("region")
    return lax.ppermute(block, "region", [(i, (i + distance) % bands) for i in range(bands)])


def shift_and_swap(block, distance):
    bands = lax.axis_size("region")
    route = [(2 * i + y, (i + distance) % bands * 2 + 1 - y) for i in range(bands) for y in (0, 1)]
    return lax.ppermute(block, ("region", "yl"), route)


def encode(blocks):
    most = jnp.max(jnp.abs(blocks), axis=(0, 1), keepdims=True)
    code = jnp.ceil(jnp.log2(jnp.maximum(most, 1e-37)) * 64.0)
    share = jnp.clip(jnp.round(blocks * jnp.exp2(code / -64.0) * 32767.0), -32767.0, 32767.0)
    return share.astype(jnp.int16), code[0].astype(jnp.int16)


def decode(share, code):
    return share.astype(jnp.float32) * (jnp.exp2(code.astype(jnp.float32) / 64.0) / 32767.0)


def carry(send, share, code):
    tile = code.shape[-2:]
    moved = send(jnp.concatenate([share.reshape(-1, *tile), code]))
    return decode(moved[:-1], moved[-1]).reshape(share.shape)


def local(tables, object_real, object_imag, probe_real, probe_imag, patterns, offsets, counts):
    slices, rows, columns = object_real.shape
    width = probe_real.shape[0]
    halves = columns // width
    depth = lax.axis_size("z")
    below = width // (4 * rows)
    packed = slices * halves * 2 * rows
    place = jnp.stack([lax.axis_index("yl"), lax.axis_index("core")]).astype(jnp.int32)
    scale = 1.0 / math.sqrt(patterns.shape[1] * depth * 4)

    with jax.named_scope("gather"):
        parts = [
            jnp.broadcast_to(
                part.reshape(slices, rows, halves, width).transpose(0, 2, 1, 3),
                (depth, slices, halves, rows, width),
            )
            for part in (object_real, object_imag)
        ]
        block = jnp.stack(parts, axis=3).reshape(depth, packed, width)
        column = lax.all_to_all(block, "z", 0, 0, tiled=True)
        column, offsets, place = lax.optimization_barrier((column, offsets, place))
        following = jnp.stack([shift(column[:below], -1), shift_and_swap(column[:below], -1)])
        own = lax.all_gather(column, ("yl", "core"), axis=0)
        following = lax.all_gather(following, "core", axis=0)

    keep, send = slots_call(
        scale, place, offsets, counts, (probe_real, probe_imag), patterns[0], tables, own, following
    )

    with jax.named_scope("reduce"):
        total = keep + swap(send, "core")
        total = total.reshape(2, depth + below, -1, 2 * rows, width)
        away = jnp.concatenate([total[1], total[0, depth:]])
        share, code = encode(away)
        near_next = carry(lambda x: shift(x, 1), share[depth + below :], code)
        far_next = carry(lambda x: shift_and_swap(x, 1), share[depth : depth + below], code)
        beside = carry(lambda x: swap(x, "yl"), share[:depth], code)
        total = (total[0, :depth] + beside).at[:below].add(near_next + far_next)
        share, code = encode(total)
        code = jnp.broadcast_to(code, (depth,) + code.shape)
        parts = jnp.concatenate([share, code], axis=1).reshape(depth, -1, width)
        parts = lax.all_to_all(parts, "z", 0, 0, tiled=True)
        parts = parts.reshape(depth, -1, 2 * rows, width)
        total = decode(parts[:, :-1], parts[:, -1:]).sum(0)
        total = total.reshape(slices, halves, 2, rows, width).transpose(2, 0, 3, 1, 4)
        total = total.reshape(2, slices, rows, columns)
    return total[0], total[1]


def solution(mesh):
    fine = Mesh(mesh.devices.reshape(mesh.shape["region"], -1, 2, 2), ("region",) + POS)
    everything = ("region",) + POS
    run = jax.shard_map(
        local,
        mesh=fine,
        in_specs=(
            P(),
            P(None, everything, None),
            P(None, everything, None),
            P(),
            P(),
            P("region", POS, None, None),
            P("region", POS, None),
            P("region", POS),
        ),
        out_specs=(P(None, everything, None), P(None, everything, None)),
        check_vma=False,
    )

    def whole(object_real, object_imag, probe_real, probe_imag, patterns, offsets, counts):
        tables = jnp.asarray(block_tables(probe_real.shape[0]))
        return run(
            tables, object_real, object_imag, probe_real, probe_imag, patterns, offsets, counts
        )

    return whole
```
